32 devices in a mesh: gx: 4 (over y, x), gy: 8 (over z, core).
Axes of the slice: x: 2, y: 2, z: 4, core: 2. Of those that a mesh axis runs over, the one named last changes fastest.
Arguments:
- tiles: bfloat16 [1024, 3, 4096], P(('gx', 'gy'))
- smoother: bfloat16 [1024, 4096], P(('gx', 'gy'))
- rhs: bfloat16 [1024, 2048], P(('gx', 'gy')), may hold values from -6 to 6
- cols: int32 [1024, 3], P(('gx', 'gy')), may hold values from 0 to 1023, as said below
- agg: int32 [1024, 1], P(('gx', 'gy')), may hold values from 0 to 7; in each aligned block of 32 rows (0 to 31, 32 to 63, ...) at most 8 rows name the same one
- coarse_slot: int32 [1024, 3], P(('gx', 'gy')), may hold values from 0 to 3
Outputs:
- iterate: float32 [1024, 2048], P(('gx', 'gy'))
- coarse_residual: float32 [32, 2048], P(('gx', 'gy'))
- coarse_tiles: float32 [32, 4, 4096], P(('gx', 'gy'))
The draws below stay inside these ranges and needn't reach their ends.
Inputs may be any that keep to these rules, and one draw needn't show every extreme that they name: cols[i, 0] = i; every other slot holds a block row at most 16 away from i, and slot 2 one exactly 16 away. `agg`: in the block rows of one device at most 8 name the same aggregate.
All inputs are finite; a program needn't handle non-finite values.
Results may differ from the reference program's by a relative error of at most 0.00045.
Values may be sent and summed in bfloat16 or wider, within the bound.
A program may use at most 64 MiB of HBM per device.

```python
import math
import jax
import jax.numpy as jnp
import numpy as np
from jax import lax

TILE = 64
NRHS = 32
K = 3
KC = 4
SWEEPS = 3
RB = 32
HALO = 16
MOST = 8
NBLK = 1024
NAGG = 32
N_GX = 4
N_GY = 8


def row_scales(key):
    level = jax.random.uniform(jax.random.fold_in(key, 11), (NBLK, TILE), jnp.float32, 0.0, math.log(4.0))
    return jnp.exp(level)


def rough_field(key, shape):
    return jax.random.normal(key, shape, jnp.float32)


def draw_tiles(key, part):
    noise = rough_field(jax.random.fold_in(key, 1), (NBLK, K, TILE, TILE))
    rows_idx = jnp.arange(TILE, dtype=jnp.int32)
    eye_mat = (rows_idx[:, None] == rows_idx[None, :]).astype(jnp.float32)
    first_slot = (jnp.arange(K, dtype=jnp.int32) == 0).astype(jnp.float32)
    base = 0.05 * noise + first_slot[None, :, None, None] * eye_mat[None, None, :, :]
    scales = row_scales(key)
    full = base * scales[:, None, :, None]
    return full.reshape(NBLK, K, TILE * TILE).astype(jnp.bfloat16)


def draw_smoother(key, part):
    noise = rough_field(jax.random.fold_in(key, 2), (NBLK, TILE, TILE))
    rows_idx = jnp.arange(TILE, dtype=jnp.int32)
    eye_mat = (rows_idx[:, None] == rows_idx[None, :]).astype(jnp.float32)
    scales = row_scales(key)
    full = 0.7 * (eye_mat[None, :, :] + 0.03 * noise) / scales[:, None, :]
    return full.reshape(NBLK, TILE * TILE).astype(jnp.bfloat16)


def draw_cols(key, part):
    block_ids = jnp.arange(NBLK, dtype=jnp.int32)
    offsets = jax.random.randint(jax.random.fold_in(key, 3), (NBLK, K), -HALO, HALO + 1, dtype=jnp.int32)
    spread = jnp.clip(block_ids[:, None] + offsets, 0, NBLK - 1)
    direction = jax.random.randint(jax.random.fold_in(key, 4), (NBLK,), 0, 2, dtype=jnp.int32) * 2 - 1
    far_col = block_ids + direction * HALO
    outside = jnp.logical_or(far_col < 0, far_col >= NBLK)
    far_col = jnp.where(outside, block_ids - direction * HALO, far_col)
    slot_ids = jnp.arange(K, dtype=jnp.int32)[None, :]
    result = jnp.where(slot_ids == 0, block_ids[:, None], spread)
    result = jnp.where(slot_ids == K - 1, far_col[:, None], result)
    return result.astype(jnp.int32)


def touch_ends(values, key, low, largest):
    spot = [jax.random.randint(jax.random.fold_in(key, axis), (), 0, length) for axis, length in enumerate(values.shape)]
    main_axis = values.shape.index(max(values.shape))
    beside = spot[:main_axis] + [(spot[main_axis] + 1) % values.shape[main_axis]] + spot[main_axis + 1:]
    return values.at[tuple(spot)].set(low).at[tuple(beside)].set(largest)


def block_levels(own_key, shape, shards, low, high):
    def one(dim, parts):
        steps = jax.random.uniform(jax.random.fold_in(jax.random.fold_in(own_key, 6), dim), (parts,), jnp.float32, low / len(shards), high / len(shards))
        return jnp.repeat(jnp.exp(steps), shape[dim] // parts).reshape((-1,) + (1,) * (len(shape) - dim - 1))

    level = one(*shards[0])
    for cut in shards[1:]:
        level = level * one(*cut)
    return level


def assign_block(stream_key, own, number, rows, count, top, reach, skew):
    order = jax.random.permutation(stream_key, count)
    crowded, common = shares(count, rows * top, reach, skew, True), shares(count, rows * top, reach, skew, False)
    places = jnp.arange(count)

    def named(sizes, turn):
        used = int((sizes > 0).sum())
        fixed = max(1, used // 4)
        passed = fixed + (places - fixed + turn * (used - fixed)) % max(1, count - fixed)
        return jnp.zeros((count,), jnp.int32).at[order[jnp.where(places < fixed, places, passed)]].set(jnp.asarray(sizes, jnp.int32))

    sizes = jnp.where(number % 4 == 0, named(crowded, number // 4), named(common, number - number // 4 - 1))
    mixed = jax.random.permutation(jax.random.fold_in(own, 3), count)
    giver, sink = mixed[0:count // 2 * 2:2], mixed[1:count // 2 * 2:2]
    room = jnp.minimum(sizes[giver] - 1, reach - sizes[sink]) // 2
    room = jnp.where((giver == order[0]) | (sink == order[0]) | (sizes[sink] == 0), 0, jnp.maximum(room, 0))
    passed = jax.random.randint(jax.random.fold_in(own, 4), (count // 2,), 0, 1 << 20) % (room + 1)
    sizes = sizes.at[giver].add(-passed).at[sink].add(passed)
    items = jnp.searchsorted(jnp.cumsum(sizes), jnp.arange(rows * top), side="right").astype(jnp.int32)
    table = items.reshape(top, rows).T
    table = table[jax.random.permutation(jax.random.fold_in(own, 1), rows)]
    turn = jax.random.randint(jax.random.fold_in(own, 2), (rows, 1), 0, top)
    return jnp.take_along_axis(table, (jnp.arange(top)[None, :] + turn) % top, axis=1)


def shares(amount, total, most, slope, full):
    portions = [(1 << 20) // math.isqrt(rank ** slope) + 1 for rank in range(1, amount + 1)]
    largest = most if full else min(most, max(-(-total // amount), total * portions[0] // sum(portions)))
    least = 1 if total - largest >= amount - 1 else 0
    holding, spare = [largest] + [least] * (amount - 1), total - largest - least * (amount - 1)
    while spare > 0:
        candidates = [i for i in range(1, amount) if holding[i] < largest] or [i for i in range(1, amount) if holding[i] < most]
        whole, remaining = sum([portions[i] for i in candidates]), spare
        for i in candidates:
            extra = min(most - holding[i], max(1, remaining * portions[i] // whole), spare)
            holding[i] = holding[i] + extra
            spare = spare - extra
    return np.array(holding)


def bell_draw(own_key, shape, deviation, most, split=(), held_as=jnp.bfloat16):
    level = block_levels(own_key, shape, split, -0.22, 0.18) if split else 1.0
    array = jax.random.normal(own_key, shape, jnp.float32) * deviation * level
    return jnp.minimum(jnp.maximum(array, -most), most).astype(held_as)


def setup_inputs(seed: int = 0) -> dict:
    seeds = jax.random.split(jax.random.key(seed), 7)
    tiles = draw_tiles(jax.random.fold_in(seeds[6], 71), 0)
    smoother = draw_smoother(jax.random.fold_in(seeds[6], 71), 0)
    rhs = bell_draw(seeds[2], (NBLK, TILE * NRHS), 1.0, 6.0, ((0, 32),))
    cols = draw_cols(jax.random.fold_in(seeds[6], 71), 0)
    agg_keys = jax.random.split(jax.random.fold_in(seeds[4], 1), NBLK // RB)
    agg_turns = jax.random.permutation(jax.random.fold_in(seeds[4], 3), NBLK // RB)
    agg = jax.vmap(lambda own, number: assign_block(jax.random.fold_in(seeds[4], 2), own, number, RB, N_GY, 1, MOST, 2))(agg_keys, agg_turns).reshape((NBLK, 1))
    coarse_slot = touch_ends(jax.random.randint(seeds[5], (NBLK, K), 0, KC), jax.random.fold_in(seeds[5], 1), 0, KC - 1).astype(jnp.int32)
    return {"tiles": tiles, "smoother": smoother, "rhs": rhs, "cols": cols, "agg": agg, "coarse_slot": coarse_slot}


def apply_operator(field, tiles, cols):
    devices_total = N_GX * N_GY
    tile_blocks = tiles.reshape(devices_total, RB, K, TILE, TILE)
    col_blocks = cols.reshape(devices_total, RB, K)

    def one_block(pair):
        tile_part, col_part = pair
        picked = field[col_part]
        return jnp.einsum("ikrc,ikcj->irj", tile_part.astype(jnp.float32), picked, precision=lax.Precision.HIGHEST)

    return lax.map(one_block, (tile_blocks, col_blocks)).reshape(NBLK, TILE, NRHS)


def apply_smoother(residual, smoother):
    devices_total = N_GX * N_GY
    smooth_blocks = smoother.reshape(devices_total, RB, TILE, TILE)
    res_blocks = residual.reshape(devices_total, RB, TILE, NRHS)

    def one_block(pair):
        mat_part, res_part = pair
        return jnp.einsum("irc,icj->irj", mat_part.astype(jnp.float32), res_part, precision=lax.Precision.HIGHEST)

    return lax.map(one_block, (smooth_blocks, res_blocks)).reshape(NBLK, TILE, NRHS)


def reference(tiles, smoother, rhs, cols, agg, coarse_slot):
    source = rhs.astype(jnp.float32).reshape(NBLK, TILE, NRHS)
    iterate = jnp.zeros((NBLK, TILE, NRHS), jnp.float32)
    for sweep_index in range(SWEEPS):
        residual = source - apply_operator(iterate, tiles, cols)
        iterate = iterate + apply_smoother(residual, smoother)
    residual = source - apply_operator(iterate, tiles, cols)
    block_ids = jnp.arange(NBLK, dtype=jnp.int32)
    aggregate = (block_ids // (RB * N_GY)) * N_GY + agg[:, 0].astype(jnp.int32)
    coarse_residual = jax.ops.segment_sum(residual.reshape(NBLK, TILE * NRHS), aggregate, num_segments=NAGG)
    keys = (aggregate[:, None] * KC + coarse_slot.astype(jnp.int32)).astype(jnp.int32)
    devices_total = N_GX * N_GY
    key_blocks = keys.reshape(devices_total, RB * K)
    tile_blocks = tiles.reshape(devices_total, RB * K, TILE * TILE)

    def add_block(carry, pair):
        tile_part, key_part = pair
        return carry.at[key_part].add(tile_part.astype(jnp.float32)), None

    start = jnp.zeros((NAGG * KC, TILE * TILE), jnp.float32)
    coarse_flat, unused = lax.scan(add_block, start, (tile_blocks, key_blocks))
    coarse_tiles = coarse_flat.reshape(NAGG, KC, TILE * TILE)
    return (iterate.reshape(NBLK, TILE * NRHS), coarse_residual, coarse_tiles)
```

```python
import functools

import jax
import jax.numpy as jnp
from jax import lax
from jax.experimental import pallas as pl
from jax.experimental.pallas import tpu as pltpu
from jax.sharding import PartitionSpec as P

TILE = 64
NRHS = 32
KC = 4
SWEEPS = 3
LANES = 128
PACK = LANES // NRHS
MESH = pl.DeviceIdType.MESH


def split(value):
    high = value.astype(jnp.bfloat16)
    low = (value - high.astype(jnp.float32)).astype(jnp.bfloat16)
    return high, low


def dot(a, b):
    return jnp.dot(a, b, preferred_element_type=jnp.float32)


def kernel(
    n_gx, n_gy, rows,
    cols_ref, agg_ref, keys_ref, flat_ref, tt_ref, ss_ref, b_ref,
    x_out, cr_out, ct_out,
    xs, xh, halo, xb, rb, acc, rq, part, pair, tin, racc, rin,
    halo_send, halo_recv, pair_send, pair_recv, tile_send, tile_recv, res_send, res_recv,
):
    gx, gy = lax.axis_index("gx"), lax.axis_index("gy")
    me = gx * n_gy + gy
    total = n_gx * n_gy
    half = rows // 2
    groups = rows // PACK
    hgroups = groups // 2
    n_par = n_gy // 2
    parity, mine = lax.rem(gy, 2), lax.div(gy, 2)
    has_left, has_right = me > 0, me < total - 1
    left = (lax.div(me + total - 1, n_gy) % n_gx, lax.rem(me + total - 1, n_gy))
    right = (lax.div(me + 1, n_gy) % n_gx, lax.rem(me + 1, n_gy))
    far_left = jnp.logical_and(gy == 0, gx > 0)
    far_right = jnp.logical_and(gy == n_gy - 1, gx < n_gx - 1)

    barrier = pltpu.get_barrier_semaphore()

    def greet(d, carry):
        pl.semaphore_signal(barrier, inc=1, device_id=(gx, lax.rem(gy + d, n_gy)), device_id_type=MESH)
        return carry

    lax.fori_loop(1, n_gy, greet, 0)

    @pl.when(far_left)
    def _():
        pl.semaphore_signal(barrier, inc=1, device_id=left, device_id_type=MESH)

    @pl.when(far_right)
    def _():
        pl.semaphore_signal(barrier, inc=1, device_id=right, device_id_type=MESH)

    def halo_copy(step, side):
        groups_sent = pl.ds(0, hgroups) if side == 0 else pl.ds(hgroups, hgroups)
        return pltpu.make_async_remote_copy(
            src_ref=xh.at[step, groups_sent],
            dst_ref=halo.at[step, 1 - side],
            send_sem=halo_send.at[step, side],
            recv_sem=halo_recv.at[step, 1 - side],
            device_id=left if side == 0 else right,
            device_id_type=MESH,
        )

    def unpack(packed, first):
        for e in range(PACK):
            xb[first + e] = packed[:, e * NRHS:(e + 1) * NRHS]

    def update(step, side):
        start = side * half
        for g in range(side * hgroups, (side + 1) * hgroups):
            gained = []
            for e in range(PACK):
                i = g * PACK + e
                if step == 0:
                    gained.append(dot(ss_ref[i][:, :TILE], b_ref[i]))
                else:
                    gained.append(dot(ss_ref[i], rb[i]))
            value = jnp.concatenate(gained, axis=1)
            if step > 0:
                value = xs[step - 1, g] + value
            xs[step, g] = value
            high, low = split(value)
            xh[step, g] = jnp.concatenate([high, low], axis=0)

    def send_halo(step, side):
        @pl.when(has_left if side == 0 else has_right)
        def _():
            halo_copy(step, side).start()

    def local_part(step):
        for g in range(groups):
            unpack(xh[step, g], half + g * PACK)
        for i in range(rows):
            acc[i] = b_ref[i].astype(jnp.float32) - dot(tt_ref[i], xb[half + i])

    def receive_halo(step):
        for side in range(2):
            @pl.when(has_right if side == 0 else has_left)
            def _():
                halo_copy(step, side).wait_recv()

        for side in range(2):
            for g in range(hgroups):
                unpack(halo[step, side, g], (0 if side == 0 else half + rows) + g * PACK)

    def residual(i):
        one = cols_ref[i, 1]
        two = cols_ref[i, 2]
        return (
            acc[i]
            - dot(tt_ref[rows + i], xb[one])
            - dot(tt_ref[2 * rows + i], xb[two])
        )

    for side in range(2):
        update(0, side)
        if side == 0:
            waits = n_gy - 1 + far_left.astype(jnp.int32) + far_right.astype(jnp.int32)
            pl.semaphore_wait(barrier, waits)

            @pl.when(jnp.logical_not(has_left))
            def _():
                halo[:, 0] = jnp.zeros_like(halo[:, 0])

            @pl.when(jnp.logical_not(has_right))
            def _():
                halo[:, 1] = jnp.zeros_like(halo[:, 1])
        send_halo(0, side)

    n_keys = n_gy * KC
    slots = lax.broadcasted_iota(jnp.int32, (n_keys, 3 * rows), 0)
    chosen = jnp.where(slots == keys_ref[...], 1.0, 0.0).astype(jnp.bfloat16)
    width = 1024
    for at in range(0, TILE * TILE, width):
        sums = dot(chosen, flat_ref[:, at:at + width])
        for p in range(2):
            for q in range(n_par):
                row = (p * n_par + q) * KC
                part[p, q, :, at:at + width] = sums[row:row + KC]
    pair_copy = pltpu.make_async_remote_copy(
        src_ref=part.at[1 - parity],
        dst_ref=pair,
        send_sem=pair_send,
        recv_sem=pair_recv,
        device_id=(gx, 2 * mine + 1 - parity),
        device_id_type=MESH,
    )
    pair_copy.start()

    def tile_copy(d):
        target = lax.rem(mine + d, n_par)
        return pltpu.make_async_remote_copy(
            src_ref=part.at[parity, target],
            dst_ref=tin.at[d - 1],
            send_sem=tile_send.at[d - 1],
            recv_sem=tile_recv.at[d - 1],
            device_id=(gx, 2 * target + parity),
            device_id_type=MESH,
        )

    def res_copy(d):
        target = lax.rem(gy + d, n_gy)
        return pltpu.make_async_remote_copy(
            src_ref=racc.at[target],
            dst_ref=rin.at[d - 1],
            send_sem=res_send.at[d - 1],
            recv_sem=res_recv.at[d - 1],
            device_id=(gx, target),
            device_id_type=MESH,
        )

    def each(first, last, act):
        def one(d, carry):
            act(d)
            return carry

        lax.fori_loop(first, last, one, 0)

    for step in range(SWEEPS - 1):
        local_part(step)
        receive_halo(step)
        for i in range(rows):
            high, low = split(residual(i))
            rb[i] = jnp.concatenate([high, low], axis=0)
        for side in range(2):
            update(step + 1, side)
            send_halo(step + 1, side)
        if step == 0:
            pair_copy.wait_recv()

            def join(q):
                part[parity, q] = part[parity, q] + pair[q]

            each(0, n_par, join)
            each(1, n_par, lambda d: tile_copy(d).start())

    last = SWEEPS - 1
    for g in range(groups):
        for e in range(PACK):
            x_out[g * PACK + e] = xs[last, g, :, e * NRHS:(e + 1) * NRHS]
    local_part(last)
    receive_halo(last)
    quarter = TILE // PACK
    for i in range(rows):
        value = residual(i)
        rq[i] = jnp.concatenate([value[e * quarter:(e + 1) * quarter] for e in range(PACK)], axis=1)

    def gather(a):
        value = jnp.zeros((quarter, LANES), jnp.float32)
        for i in range(rows):
            value = value + jnp.where(agg_ref[i, 0] == a, 1.0, 0.0) * rq[i]
        racc[a] = value

    each(0, n_gy, gather)
    each(1, n_gy, lambda d: res_copy(d).start())

    ct_out[...] = part[parity, mine]

    def add_tiles(d):
        tile_copy(d).wait_recv()
        ct_out[...] = ct_out[...] + tin[d - 1]

    each(1, n_par, add_tiles)

    racc_mine = racc[gy]

    def add_res(d, value):
        res_copy(d).wait_recv()
        return value + rin[d - 1]

    final = lax.fori_loop(1, n_gy, add_res, racc_mine)
    for e in range(PACK):
        cr_out[e * quarter:(e + 1) * quarter, :] = final[:, e * NRHS:(e + 1) * NRHS]

    for step in range(SWEEPS):
        for side in range(2):
            @pl.when(has_left if side == 0 else has_right)
            def _():
                halo_copy(step, side).wait_send()
    pair_copy.wait_send()
    each(1, n_par, lambda d: tile_copy(d).wait_send())
    each(1, n_gy, lambda d: res_copy(d).wait_send())


def body(n_gx, n_gy, tiles, smoother, rhs, cols, agg, coarse_slot):
    rows = tiles.shape[0]
    n_par = n_gy // 2
    groups = rows // PACK
    flat = tiles.transpose(1, 0, 2).reshape(rows * 3, TILE * TILE)
    square = flat.reshape(rows * 3, TILE, TILE)
    double = jnp.concatenate([square, square], axis=2)
    smooth = smoother.reshape(rows, TILE, TILE)
    smooth = jnp.concatenate([smooth, smooth], axis=2)
    source = rhs.reshape(rows, TILE, NRHS)
    places = cols - (lax.axis_index(("gx", "gy")) * rows - rows // 2)
    order = (agg % 2) * n_par + agg // 2
    keys = (order * KC + coarse_slot).T.reshape(1, rows * 3)
    vmem = pl.BlockSpec(memory_space=pltpu.VMEM)
    smem = pl.BlockSpec(memory_space=pltpu.SMEM)
    quarter = TILE // PACK
    f32, bf16 = jnp.float32, jnp.bfloat16
    dma = pltpu.SemaphoreType.DMA
    iterate, residual, coarse = pl.pallas_call(
        functools.partial(kernel, n_gx, n_gy, rows),
        out_shape=(
            jax.ShapeDtypeStruct((rows, TILE, NRHS), f32),
            jax.ShapeDtypeStruct((TILE, NRHS), f32),
            jax.ShapeDtypeStruct((KC, TILE * TILE), f32),
        ),
        in_specs=[smem, smem, vmem, vmem, vmem, vmem, vmem],
        out_specs=(vmem, vmem, vmem),
        scratch_shapes=[
            pltpu.VMEM((SWEEPS, groups, TILE, LANES), f32),
            pltpu.VMEM((SWEEPS, groups, 2 * TILE, LANES), bf16),
            pltpu.VMEM((SWEEPS, 2, groups // 2, 2 * TILE, LANES), bf16),
            pltpu.VMEM((2 * rows, 2 * TILE, NRHS), bf16),
            pltpu.VMEM((rows, 2 * TILE, NRHS), bf16),
            pltpu.VMEM((rows, TILE, NRHS), f32),
            pltpu.VMEM((rows, quarter, LANES), f32),
            pltpu.VMEM((2, n_par, KC, TILE * TILE), f32),
            pltpu.VMEM((n_par, KC, TILE * TILE), f32),
            pltpu.VMEM((n_par - 1, KC, TILE * TILE), f32),
            pltpu.VMEM((n_gy, quarter, LANES), f32),
            pltpu.VMEM((n_gy - 1, quarter, LANES), f32),
            dma((SWEEPS, 2)), dma((SWEEPS, 2)), dma, dma,
            dma((n_par - 1,)), dma((n_par - 1,)), dma((n_gy - 1,)), dma((n_gy - 1,)),
        ],
        compiler_params=pltpu.CompilerParams(
            collective_id=0, has_side_effects=True, vmem_limit_bytes=50 * 1024 * 1024
        ),
    )(places, agg, keys, flat, double, smooth, source)
    return (
        iterate.reshape(rows, TILE * NRHS),
        residual.reshape(1, TILE * NRHS),
        coarse.reshape(1, KC, TILE * TILE),
    )


def solution(mesh):
    row_spec = P(("gx", "gy"), None)
    tile_spec = P(("gx", "gy"), None, None)
    return jax.shard_map(
        functools.partial(body, mesh.shape["gx"], mesh.shape["gy"]),
        mesh=mesh,
        in_specs=(tile_spec, row_spec, row_spec, row_spec, row_spec, row_spec),
        out_specs=(row_spec, row_spec, tile_spec),
        check_vma=False,
    )
```

```python
import functools

import jax
import jax.numpy as jnp
from jax import lax
from jax.experimental import pallas as pl
from jax.experimental.pallas import tpu as pltpu
from jax.sharding import PartitionSpec as P

TILE = 64
NRHS = 32
KC = 4
SWEEPS = 3
LANES = 128
PITCH = 72
PACK = LANES // NRHS
MESH = pl.DeviceIdType.MESH


def split(value):
    high = value.astype(jnp.bfloat16)
    low = (value - high.astype(jnp.float32)).astype(jnp.bfloat16)
    return high, low


def dot(a, b):
    return jnp.dot(a, b, preferred_element_type=jnp.float32)


def kernel(
    n_gx, n_gy, rows,
    cols_ref, agg_ref, keys_ref, flat_ref, smooth_ref, rhs_ref,
    x_out, cr_out, ct_out,
    ts, fs, bs, xf, tt, ss, xs, xh, halo, xb, rb, acc, rq, part, pair, tin, racc, rin,
    halo_send, halo_recv, pair_send, pair_recv, tile_send, tile_recv, res_send, res_recv,
):
    gx, gy = lax.axis_index("gx"), lax.axis_index("gy")
    me = gx * n_gy + gy
    total = n_gx * n_gy
    half = rows // 2
    groups = rows // PACK
    hgroups = groups // 2
    n_par = n_gy // 2
    parity, mine = lax.rem(gy, 2), lax.div(gy, 2)
    has_left, has_right = me > 0, me < total - 1
    left = (lax.div(me + total - 1, n_gy) % n_gx, lax.rem(me + total - 1, n_gy))
    right = (lax.div(me + 1, n_gy) % n_gx, lax.rem(me + 1, n_gy))
    far_left = jnp.logical_and(gy == 0, gx > 0)
    far_right = jnp.logical_and(gy == n_gy - 1, gx < n_gx - 1)

    barrier = pltpu.get_barrier_semaphore()

    def greet(d, carry):
        pl.semaphore_signal(barrier, inc=1, device_id=(gx, lax.rem(gy + d, n_gy)), device_id_type=MESH)
        return carry

    lax.fori_loop(1, n_gy, greet, 0)

    @pl.when(far_left)
    def _():
        pl.semaphore_signal(barrier, inc=1, device_id=left, device_id_type=MESH)

    @pl.when(far_right)
    def _():
        pl.semaphore_signal(barrier, inc=1, device_id=right, device_id_type=MESH)

    def each(first, last, act):
        def one(d, carry):
            act(d)
            return carry

        lax.fori_loop(first, last, one, 0)

    def square(source, count, spread, target):
        low_lanes = lax.broadcasted_iota(jnp.int32, (count, LANES), 1) < TILE
        for p in range(TILE // 2):
            strip = source[:, LANES * p:LANES * (p + 1)].astype(jnp.float32)
            turned = pltpu.roll(strip, TILE, 1)
            spread[pl.ds(2 * p, count, stride=PITCH), :] = jnp.where(low_lanes, strip, turned)
            spread[pl.ds(2 * p + 1, count, stride=PITCH), :] = jnp.where(low_lanes, turned, strip)
        for t in range(count):
            target[t] = spread[PITCH * t:PITCH * t + TILE, :].astype(jnp.bfloat16)

    def source_block(i):
        return bs[PITCH * i:PITCH * i + TILE, :NRHS]

    def halo_copy(step, side, g):
        return pltpu.make_async_remote_copy(
            src_ref=xh.at[step, side * hgroups + g],
            dst_ref=halo.at[step, 1 - side, g],
            send_sem=halo_send.at[step, side, g],
            recv_sem=halo_recv.at[step, 1 - side, g],
            device_id=left if side == 0 else right,
            device_id_type=MESH,
        )

    def unpack(buffer, packed, first):
        for e in range(PACK):
            xb[buffer, first + e] = packed[:, e * NRHS:(e + 1) * NRHS]

    def update(step, side, g):
        gained = []
        for e in range(PACK):
            i = g * PACK + e
            if step == 0:
                gained.append(dot(ss[i][:, :TILE], source_block(i).astype(jnp.bfloat16)))
            else:
                gained.append(dot(ss[i], rb[i]))
        value = jnp.concatenate(gained, axis=1)
        if step > 0:
            value = xs[step - 1, g] + value
        xs[step, g] = value
        high, low = split(value)
        packed = jnp.concatenate([high, low], axis=0)
        xh[step, g] = packed
        unpack(step % 2, packed, half + g * PACK)
        if step == SWEEPS - 1:
            for e in range(PACK):
                first = PITCH * (g * PACK + e)
                xf[first:first + TILE, :NRHS] = value[:, e * NRHS:(e + 1) * NRHS]

    def update_side(step, side):
        for g in range(hgroups):
            update(step, side, side * hgroups + g)

            @pl.when(has_left if side == 0 else has_right)
            def _():
                halo_copy(step, side, g).start()

    def local_part(step, side):
        for i in range(side * half, (side + 1) * half):
            acc[i] = source_block(i) - dot(tt[i], xb[step % 2, half + i])

    def receive_halo(step, side):
        for g in range(hgroups):
            @pl.when(has_left if side == 0 else has_right)
            def _():
                halo_copy(step, 1 - side, g).wait_recv()

        for g in range(hgroups):
            unpack(step % 2, halo[step, side, g], (0 if side == 0 else half + rows) + g * PACK)

    def residual(step, i):
        one = cols_ref[i, 1]
        two = cols_ref[i, 2]
        return (
            acc[i]
            - dot(tt[rows + i], xb[step % 2, one])
            - dot(tt[2 * rows + i], xb[step % 2, two])
        )

    low_lanes = lax.broadcasted_iota(jnp.int32, (rows, LANES), 1)
    for q in range(TILE // PACK):
        strip = rhs_ref[:, LANES * q:LANES * (q + 1)].astype(jnp.float32)
        for e in range(PACK):
            turned = strip if e == 0 else pltpu.roll(strip, LANES - NRHS * e, 1)
            bs[pl.ds(PACK * q + e, rows, stride=PITCH), :] = turned
    square(smooth_ref, rows, fs, ss)

    waits = n_gy - 1 + far_left.astype(jnp.int32) + far_right.astype(jnp.int32)
    pl.semaphore_wait(barrier, waits)
    update_side(0, 0)
    update_side(0, 1)

    @pl.when(jnp.logical_not(has_left))
    def _():
        halo[:, 0] = jnp.zeros_like(halo[:, 0])

    @pl.when(jnp.logical_not(has_right))
    def _():
        halo[:, 1] = jnp.zeros_like(halo[:, 1])

    square(flat_ref, 3 * rows, ts, tt)

    n_keys = n_gy * KC
    slots = lax.broadcasted_iota(jnp.int32, (n_keys, 3 * rows), 0)
    chosen = jnp.where(slots == keys_ref[...], 1.0, 0.0).astype(jnp.bfloat16)
    width = 1024
    for at in range(0, TILE * TILE, width):
        sums = dot(chosen, flat_ref[:, at:at + width])
        for p in range(2):
            for q in range(n_par):
                row = (p * n_par + q) * KC
                part[p, q, :, at:at + width] = sums[row:row + KC]
    pair_copy = pltpu.make_async_remote_copy(
        src_ref=part.at[1 - parity],
        dst_ref=pair,
        send_sem=pair_send,
        recv_sem=pair_recv,
        device_id=(gx, 2 * mine + 1 - parity),
        device_id_type=MESH,
    )
    pair_copy.start()

    def tile_copy(d):
        target = lax.rem(mine + d, n_par)
        return pltpu.make_async_remote_copy(
            src_ref=part.at[parity, target],
            dst_ref=tin.at[d - 1],
            send_sem=tile_send.at[d - 1],
            recv_sem=tile_recv.at[d - 1],
            device_id=(gx, 2 * target + parity),
            device_id_type=MESH,
        )

    def res_copy(d):
        target = lax.rem(gy + d, n_gy)
        return pltpu.make_async_remote_copy(
            src_ref=racc.at[target],
            dst_ref=rin.at[d - 1],
            send_sem=res_send.at[d - 1],
            recv_sem=res_recv.at[d - 1],
            device_id=(gx, target),
            device_id_type=MESH,
        )

    for side in range(2):
        local_part(0, side)
    for step in range(SWEEPS - 1):
        for side in ((1, 0) if step % 2 == 0 else (0, 1)):
            receive_halo(step, side)
            for i in range(side * half, (side + 1) * half):
                high, low = split(residual(step, i))
                rb[i] = jnp.concatenate([high, low], axis=0)
            update_side(step + 1, side)
        if step == 0:
            pair_copy.wait_recv()

            def join(q):
                part[parity, q] = part[parity, q] + pair[q]

            each(0, n_par, join)
            each(1, n_par, lambda d: tile_copy(d).start())
        for side in range(2):
            local_part(step + 1, side)

    last = SWEEPS - 1
    for q in range(TILE // PACK):
        strips = [xf[pl.ds(PACK * q + e, rows, stride=PITCH), :][:, :NRHS] for e in range(PACK)]
        x_out[:, LANES * q:LANES * (q + 1)] = jnp.concatenate(strips, axis=1)
    ct_out[...] = part[parity, mine]

    def add_tiles(d):
        tile_copy(d).wait_recv()
        ct_out[...] = ct_out[...] + tin[d - 1]

    each(1, n_par, add_tiles)

    quarter = TILE // PACK
    for side in ((1, 0) if last % 2 == 0 else (0, 1)):
        receive_halo(last, side)
        for i in range(side * half, (side + 1) * half):
            value = residual(last, i)
            rq[i] = jnp.concatenate([value[e * quarter:(e + 1) * quarter] for e in range(PACK)], axis=1)

    def gather(a):
        value = jnp.zeros((quarter, LANES), jnp.float32)
        for i in range(rows):
            value = value + jnp.where(agg_ref[i, 0] == a, 1.0, 0.0) * rq[i]
        racc[a] = value

    def gather_send(d):
        gather(lax.rem(gy + d, n_gy))
        res_copy(d).start()

    each(1, n_gy, gather_send)
    gather(gy)

    def add_res(d, value):
        res_copy(d).wait_recv()
        return value + rin[d - 1]

    final = lax.fori_loop(1, n_gy, add_res, racc[gy])
    for e in range(PACK):
        xf[e * quarter:(e + 1) * quarter, :NRHS] = final[:, e * NRHS:(e + 1) * NRHS]
    strips = [xf[pl.ds(e, quarter, stride=PACK), :][:, :NRHS] for e in range(PACK)]
    cr_out[...] = jnp.concatenate(strips, axis=1)

    for step in range(SWEEPS):
        for side in range(2):
            for g in range(hgroups):
                @pl.when(has_left if side == 0 else has_right)
                def _():
                    halo_copy(step, side, g).wait_send()
    pair_copy.wait_send()
    each(1, n_par, lambda d: tile_copy(d).wait_send())
    each(1, n_gy, lambda d: res_copy(d).wait_send())


def body(n_gx, n_gy, tiles, smoother, rhs, cols, agg, coarse_slot):
    rows = tiles.shape[0]
    n_par = n_gy // 2
    groups = rows // PACK
    flat = tiles.transpose(1, 0, 2).reshape(rows * 3, TILE * TILE)
    places = cols - (lax.axis_index(("gx", "gy")) * rows - rows // 2)
    order = (agg % 2) * n_par + agg // 2
    keys = (order * KC + coarse_slot).T.reshape(1, rows * 3)
    vmem = pl.BlockSpec(memory_space=pltpu.VMEM)
    smem = pl.BlockSpec(memory_space=pltpu.SMEM)
    quarter = TILE // PACK
    f32, bf16 = jnp.float32, jnp.bfloat16
    dma = pltpu.SemaphoreType.DMA
    iterate, residual, coarse = pl.pallas_call(
        functools.partial(kernel, n_gx, n_gy, rows),
        out_shape=(
            jax.ShapeDtypeStruct((rows, TILE * NRHS), f32),
            jax.ShapeDtypeStruct((quarter, LANES), f32),
            jax.ShapeDtypeStruct((KC, TILE * TILE), f32),
        ),
        in_specs=[smem, smem, vmem, vmem, vmem, vmem],
        out_specs=(vmem, vmem, vmem),
        scratch_shapes=[
            pltpu.VMEM((3 * rows * PITCH, LANES), f32),
            pltpu.VMEM((rows * PITCH, LANES), f32),
            pltpu.VMEM((rows * PITCH, LANES), f32),
            pltpu.VMEM((rows * PITCH, LANES), f32),
            pltpu.VMEM((3 * rows, TILE, LANES), bf16),
            pltpu.VMEM((rows, TILE, LANES), bf16),
            pltpu.VMEM((SWEEPS, groups, TILE, LANES), f32),
            pltpu.VMEM((SWEEPS, groups, 2 * TILE, LANES), bf16),
            pltpu.VMEM((SWEEPS, 2, groups // 2, 2 * TILE, LANES), bf16),
            pltpu.VMEM((2, 2 * rows, 2 * TILE, NRHS), bf16),
            pltpu.VMEM((rows, 2 * TILE, NRHS), bf16),
            pltpu.VMEM((rows, TILE, NRHS), f32),
            pltpu.VMEM((rows, quarter, LANES), f32),
            pltpu.VMEM((2, n_par, KC, TILE * TILE), f32),
            pltpu.VMEM((n_par, KC, TILE * TILE), f32),
            pltpu.VMEM((n_par - 1, KC, TILE * TILE), f32),
            pltpu.VMEM((n_gy, quarter, LANES), f32),
            pltpu.VMEM((n_gy - 1, quarter, LANES), f32),
            dma((SWEEPS, 2, groups // 2)), dma((SWEEPS, 2, groups // 2)), dma, dma,
            dma((n_par - 1,)), dma((n_par - 1,)), dma((n_gy - 1,)), dma((n_gy - 1,)),
        ],
        compiler_params=pltpu.CompilerParams(
            collective_id=0, has_side_effects=True, vmem_limit_bytes=50 * 1024 * 1024
        ),
    )(places, agg, keys, flat, smoother, rhs)
    return (
        iterate,
        residual.reshape(1, TILE * NRHS),
        coarse.reshape(1, KC, TILE * TILE),
    )


def solution(mesh):
    row_spec = P(("gx", "gy"), None)
    tile_spec = P(("gx", "gy"), None, None)
    return jax.shard_map(
        functools.partial(body, mesh.shape["gx"], mesh.shape["gy"]),
        mesh=mesh,
        in_specs=(tile_spec, row_spec, row_spec, row_spec, row_spec, row_spec),
        out_specs=(row_spec, row_spec, tile_spec),
        check_vma=False,
    )
```

```python
import functools

import jax
import jax.numpy as jnp
from jax import lax
from jax.experimental import pallas as pl
from jax.experimental.pallas import tpu as pltpu
from jax.sharding import PartitionSpec as P

TILE = 64
NRHS = 32
KC = 4
SWEEPS = 3
LANES = 128
PITCH = 72
PACK = LANES // NRHS
MESH = pl.DeviceIdType.MESH


def split(value):
    high = value.astype(jnp.bfloat16)
    low = (value - high.astype(jnp.float32)).astype(jnp.bfloat16)
    return high, low


def dot(a, b):
    return jnp.dot(a, b, preferred_element_type=jnp.float32)


def kernel(
    n_gx, n_gy, rows,
    cols_ref, agg_ref, keys_ref, flat_hbm, smooth_hbm, rhs_hbm,
    x_out, cr_out, ct_out,
    flat_ref, smooth_ref, rhs_ref, load_sem, ts, fs, bs, xf, tt, ss, xs, xh, halo, xb, rb, acc, rq, part, pair, tin, racc, rin,
    halo_send, halo_recv, pair_send, pair_recv, tile_send, tile_recv, res_send, res_recv,
):
    gx, gy = lax.axis_index("gx"), lax.axis_index("gy")
    me = gx * n_gy + gy
    total = n_gx * n_gy
    half = rows // 2
    groups = rows // PACK
    hgroups = groups // 2
    n_par = n_gy // 2
    parity, mine = lax.rem(gy, 2), lax.div(gy, 2)
    has_left, has_right = me > 0, me < total - 1
    left = (lax.div(me + total - 1, n_gy) % n_gx, lax.rem(me + total - 1, n_gy))
    right = (lax.div(me + 1, n_gy) % n_gx, lax.rem(me + 1, n_gy))
    far_left = jnp.logical_and(gy == 0, gx > 0)
    far_right = jnp.logical_and(gy == n_gy - 1, gx < n_gx - 1)

    rhs_load = pltpu.make_async_copy(rhs_hbm, rhs_ref, load_sem.at[0])
    smooth_load = pltpu.make_async_copy(smooth_hbm, smooth_ref, load_sem.at[1])
    flat_load = pltpu.make_async_copy(flat_hbm, flat_ref, load_sem.at[2])
    rhs_load.start()
    smooth_load.start()
    flat_load.start()
    barrier = pltpu.get_barrier_semaphore()

    def greet(d, carry):
        pl.semaphore_signal(barrier, inc=1, device_id=(gx, lax.rem(gy + d, n_gy)), device_id_type=MESH)
        return carry

    lax.fori_loop(1, n_gy, greet, 0)

    @pl.when(far_left)
    def _():
        pl.semaphore_signal(barrier, inc=1, device_id=left, device_id_type=MESH)

    @pl.when(far_right)
    def _():
        pl.semaphore_signal(barrier, inc=1, device_id=right, device_id_type=MESH)

    def each(first, last, act):
        def one(d, carry):
            act(d)
            return carry

        lax.fori_loop(first, last, one, 0)

    def square(source, count, spread, target):
        low_lanes = lax.broadcasted_iota(jnp.int32, (count, LANES), 1) < TILE
        for p in range(TILE // 2):
            strip = source[:, LANES * p:LANES * (p + 1)].astype(jnp.float32)
            turned = pltpu.roll(strip, TILE, 1)
            spread[pl.ds(2 * p, count, stride=PITCH), :] = jnp.where(low_lanes, strip, turned)
            spread[pl.ds(2 * p + 1, count, stride=PITCH), :] = jnp.where(low_lanes, turned, strip)
        for t in range(count):
            target[t] = spread[PITCH * t:PITCH * t + TILE, :].astype(jnp.bfloat16)

    def source_block(i):
        return bs[PITCH * i:PITCH * i + TILE, :NRHS]

    def halo_copy(step, side, g):
        return pltpu.make_async_remote_copy(
            src_ref=xh.at[step, side * hgroups + g],
            dst_ref=halo.at[step, 1 - side, g],
            send_sem=halo_send.at[step, side, g],
            recv_sem=halo_recv.at[step, 1 - side, g],
            device_id=left if side == 0 else right,
            device_id_type=MESH,
        )

    def unpack(buffer, packed, first):
        for e in range(PACK):
            xb[buffer, first + e] = packed[:, e * NRHS:(e + 1) * NRHS]

    def update(step, side, g):
        gained = []
        for e in range(PACK):
            i = g * PACK + e
            if step == 0:
                gained.append(dot(ss[i][:, :TILE], source_block(i).astype(jnp.bfloat16)))
            else:
                gained.append(dot(ss[i], rb[i]))
        value = jnp.concatenate(gained, axis=1)
        if step > 0:
            value = xs[step - 1, g] + value
        xs[step, g] = value
        high, low = split(value)
        packed = jnp.concatenate([high, low], axis=0)
        xh[step, g] = packed
        unpack(step % 2, packed, half + g * PACK)
        if step == SWEEPS - 1:
            for e in range(PACK):
                first = PITCH * (g * PACK + e)
                xf[first:first + TILE, :NRHS] = value[:, e * NRHS:(e + 1) * NRHS]

    def update_side(step, side):
        for g in range(hgroups):
            update(step, side, side * hgroups + g)

            @pl.when(has_left if side == 0 else has_right)
            def _():
                halo_copy(step, side, g).start()

    def local_part(step, side):
        for i in range(side * half, (side + 1) * half):
            acc[i] = source_block(i) - dot(tt[i], xb[step % 2, half + i])

    def receive_halo(step, side):
        for g in range(hgroups):
            @pl.when(has_left if side == 0 else has_right)
            def _():
                halo_copy(step, 1 - side, g).wait_recv()

        for g in range(hgroups):
            unpack(step % 2, halo[step, side, g], (0 if side == 0 else half + rows) + g * PACK)

    def residual(step, i):
        one = cols_ref[i, 1]
        two = cols_ref[i, 2]
        return (
            acc[i]
            - dot(tt[rows + i], xb[step % 2, one])
            - dot(tt[2 * rows + i], xb[step % 2, two])
        )

    rhs_load.wait()
    for q in range(TILE // PACK):
        strip = rhs_ref[:, LANES * q:LANES * (q + 1)].astype(jnp.float32)
        for e in range(PACK):
            turned = strip if e == 0 else pltpu.roll(strip, LANES - NRHS * e, 1)
            bs[pl.ds(PACK * q + e, rows, stride=PITCH), :] = turned
    smooth_load.wait()
    square(smooth_ref, rows, fs, ss)

    waits = n_gy - 1 + far_left.astype(jnp.int32) + far_right.astype(jnp.int32)
    pl.semaphore_wait(barrier, waits)
    update_side(0, 0)
    update_side(0, 1)

    @pl.when(jnp.logical_not(has_left))
    def _():
        halo[:, 0] = jnp.zeros_like(halo[:, 0])

    @pl.when(jnp.logical_not(has_right))
    def _():
        halo[:, 1] = jnp.zeros_like(halo[:, 1])

    flat_load.wait()
    square(flat_ref, 3 * rows, ts, tt)

    n_keys = n_gy * KC
    slots = lax.broadcasted_iota(jnp.int32, (n_keys, 3 * rows), 0)
    chosen = jnp.where(slots == keys_ref[...], 1.0, 0.0).astype(jnp.bfloat16)
    width = 1024
    for at in range(0, TILE * TILE, width):
        sums = dot(chosen, flat_ref[:, at:at + width])
        for p in range(2):
            for q in range(n_par):
                row = (p * n_par + q) * KC
                part[p, q, :, at:at + width] = sums[row:row + KC]
    pair_copy = pltpu.make_async_remote_copy(
        src_ref=part.at[1 - parity],
        dst_ref=pair,
        send_sem=pair_send,
        recv_sem=pair_recv,
        device_id=(gx, 2 * mine + 1 - parity),
        device_id_type=MESH,
    )
    pair_copy.start()

    def tile_copy(d):
        target = lax.rem(mine + d, n_par)
        return pltpu.make_async_remote_copy(
            src_ref=part.at[parity, target],
            dst_ref=tin.at[d - 1],
            send_sem=tile_send.at[d - 1],
            recv_sem=tile_recv.at[d - 1],
            device_id=(gx, 2 * target + parity),
            device_id_type=MESH,
        )

    def res_copy(d):
        target = lax.rem(gy + d, n_gy)
        return pltpu.make_async_remote_copy(
            src_ref=racc.at[target],
            dst_ref=rin.at[d - 1],
            send_sem=res_send.at[d - 1],
            recv_sem=res_recv.at[d - 1],
            device_id=(gx, target),
            device_id_type=MESH,
        )

    for side in range(2):
        local_part(0, side)
    for step in range(SWEEPS - 1):
        for side in ((1, 0) if step % 2 == 0 else (0, 1)):
            receive_halo(step, side)
            for i in range(side * half, (side + 1) * half):
                high, low = split(residual(step, i))
                rb[i] = jnp.concatenate([high, low], axis=0)
            update_side(step + 1, side)
        if step == 0:
            pair_copy.wait_recv()

            def join(q):
                part[parity, q] = part[parity, q] + pair[q]

            each(0, n_par, join)
            each(1, n_par, lambda d: tile_copy(d).start())
        for side in range(2):
            local_part(step + 1, side)

    last = SWEEPS - 1
    for q in range(TILE // PACK):
        strips = [xf[pl.ds(PACK * q + e, rows, stride=PITCH), :][:, :NRHS] for e in range(PACK)]
        x_out[:, LANES * q:LANES * (q + 1)] = jnp.concatenate(strips, axis=1)
    ct_out[...] = part[parity, mine]

    def add_tiles(d):
        tile_copy(d).wait_recv()
        ct_out[...] = ct_out[...] + tin[d - 1]

    each(1, n_par, add_tiles)

    quarter = TILE // PACK
    for side in ((1, 0) if last % 2 == 0 else (0, 1)):
        receive_halo(last, side)
        for i in range(side * half, (side + 1) * half):
            value = residual(last, i)
            rq[i] = jnp.concatenate([value[e * quarter:(e + 1) * quarter] for e in range(PACK)], axis=1)

    def gather(a):
        value = jnp.zeros((quarter, LANES), jnp.float32)
        for i in range(rows):
            value = value + jnp.where(agg_ref[i, 0] == a, 1.0, 0.0) * rq[i]
        racc[a] = value

    def gather_send(d):
        gather(lax.rem(gy + d, n_gy))
        res_copy(d).start()

    each(1, n_gy, gather_send)
    gather(gy)

    def add_res(d, value):
        res_copy(d).wait_recv()
        return value + rin[d - 1]

    final = lax.fori_loop(1, n_gy, add_res, racc[gy])
    for e in range(PACK):
        xf[e * quarter:(e + 1) * quarter, :NRHS] = final[:, e * NRHS:(e + 1) * NRHS]
    strips = [xf[pl.ds(e, quarter, stride=PACK), :][:, :NRHS] for e in range(PACK)]
    cr_out[...] = jnp.concatenate(strips, axis=1)

    for step in range(SWEEPS):
        for side in range(2):
            for g in range(hgroups):
                @pl.when(has_left if side == 0 else has_right)
                def _():
                    halo_copy(step, side, g).wait_send()
    pair_copy.wait_send()
    each(1, n_par, lambda d: tile_copy(d).wait_send())
    each(1, n_gy, lambda d: res_copy(d).wait_send())


def body(n_gx, n_gy, tiles, smoother, rhs, cols, agg, coarse_slot):
    rows = tiles.shape[0]
    n_par = n_gy // 2
    groups = rows // PACK
    flat = tiles.transpose(1, 0, 2).reshape(rows * 3, TILE * TILE)
    places = cols - (lax.axis_index(("gx", "gy")) * rows - rows // 2)
    order = (agg % 2) * n_par + agg // 2
    keys = (order * KC + coarse_slot).T.reshape(1, rows * 3)
    vmem = pl.BlockSpec(memory_space=pltpu.VMEM)
    hbm = pl.BlockSpec(memory_space=pltpu.HBM)
    smem = pl.BlockSpec(memory_space=pltpu.SMEM)
    quarter = TILE // PACK
    f32, bf16 = jnp.float32, jnp.bfloat16
    dma = pltpu.SemaphoreType.DMA
    iterate, residual, coarse = pl.pallas_call(
        functools.partial(kernel, n_gx, n_gy, rows),
        out_shape=(
            jax.ShapeDtypeStruct((rows, TILE * NRHS), f32),
            jax.ShapeDtypeStruct((quarter, LANES), f32),
            jax.ShapeDtypeStruct((KC, TILE * TILE), f32),
        ),
        in_specs=[smem, smem, vmem, hbm, hbm, hbm],
        out_specs=(vmem, vmem, vmem),
        scratch_shapes=[
            pltpu.VMEM((3 * rows, TILE * TILE), bf16),
            pltpu.VMEM((rows, TILE * TILE), bf16),
            pltpu.VMEM((rows, TILE * NRHS), bf16),
            dma((3,)),
            pltpu.VMEM((3 * rows * PITCH, LANES), f32),
            pltpu.VMEM((rows * PITCH, LANES), f32),
            pltpu.VMEM((rows * PITCH, LANES), f32),
            pltpu.VMEM((rows * PITCH, LANES), f32),
            pltpu.VMEM((3 * rows, TILE, LANES), bf16),
            pltpu.VMEM((rows, TILE, LANES), bf16),
            pltpu.VMEM((SWEEPS, groups, TILE, LANES), f32),
            pltpu.VMEM((SWEEPS, groups, 2 * TILE, LANES), bf16),
            pltpu.VMEM((SWEEPS, 2, groups // 2, 2 * TILE, LANES), bf16),
            pltpu.VMEM((2, 2 * rows, 2 * TILE, NRHS), bf16),
            pltpu.VMEM((rows, 2 * TILE, NRHS), bf16),
            pltpu.VMEM((rows, TILE, NRHS), f32),
            pltpu.VMEM((rows, quarter, LANES), f32),
            pltpu.VMEM((2, n_par, KC, TILE * TILE), f32),
            pltpu.VMEM((n_par, KC, TILE * TILE), f32),
            pltpu.VMEM((n_par - 1, KC, TILE * TILE), f32),
            pltpu.VMEM((n_gy, quarter, LANES), f32),
            pltpu.VMEM((n_gy - 1, quarter, LANES), f32),
            dma((SWEEPS, 2, groups // 2)), dma((SWEEPS, 2, groups // 2)), dma, dma,
            dma((n_par - 1,)), dma((n_par - 1,)), dma((n_gy - 1,)), dma((n_gy - 1,)),
        ],
        compiler_params=pltpu.CompilerParams(
            collective_id=0, has_side_effects=True, vmem_limit_bytes=63 * 1024 * 1024
        ),
    )(places, agg, keys, flat, smoother, rhs)
    return (
        iterate,
        residual.reshape(1, TILE * NRHS),
        coarse.reshape(1, KC, TILE * TILE),
    )


def solution(mesh):
    row_spec = P(("gx", "gy"), None)
    tile_spec = P(("gx", "gy"), None, None)
    return jax.shard_map(
        functools.partial(body, mesh.shape["gx"], mesh.shape["gy"]),
        mesh=mesh,
        in_specs=(tile_spec, row_spec, row_spec, row_spec, row_spec, row_spec),
        out_specs=(row_spec, row_spec, tile_spec),
        check_vma=False,
    )
```
